32 devices in a mesh: freq: 8 (over z, x), rcv: 4 (over y, core).
Axes of the slice: x: 2, y: 2, z: 4, core: 2. Of those that a mesh axis runs over, the one named last changes fastest.
Arguments:
- primaries_start: float32 [512, 1024, 128], P(('rcv', 'freq')), may hold values from -6 to 6
- surface_operator: bfloat16 [512, 2, 384, 512], P('freq', None, 'rcv'), may hold values from -0.25 to 0.25
- data_spectra: bfloat16 [384, 512, 2, 128], P('rcv', 'freq'), may hold values from -6 to 6
- shrinkage: float32 [128], replicated, may hold values from 0.2 to 2
Outputs:
- primaries: float32 [512, 1024, 128], P(('rcv', 'freq'))
- residual_spectra: bfloat16 [384, 512, 2, 128], P('rcv', 'freq')
The draws below stay inside these ranges and needn't reach their ends.
All inputs are finite; a program needn't handle non-finite values.
Results may differ from the reference program's by a relative error of at most 0.0085.
Values may be sent and summed in bfloat16 or wider, within the bound.
A program may use at most 192 MiB of HBM per device.

```python
import math
import jax
import jax.numpy as jnp
from jax import lax

S = 128
NS = 512
R = 384
T_SIZE = 1024
ITERS = 2
NF = 512


def strengthened(drawn, key, source, target, shards_of, factor):
    owner, partner = [(jnp.arange(drawn.shape[position]) // (drawn.shape[position] // shards_of)).reshape([-1 if axis == position else 1 for axis in range(drawn.ndim)]) for position in (source, target)]
    chosen = jax.random.permutation(key, shards_of)[partner]
    strong = (owner == chosen) | (owner == (partner + shards_of // 2) % shards_of)
    return jnp.where(strong, factor * drawn, drawn)


def block_scale(own_key, dims, pieces, least, top_value):
    factor_of = 1.0
    for dim, parts in pieces:
        steps = jax.random.uniform(jax.random.fold_in(jax.random.fold_in(own_key, 6), dim), (parts,), jnp.float32, least / len(pieces), top_value / len(pieces))
        factor_of = factor_of * jnp.repeat(jnp.exp(steps), dims[dim] // parts).reshape((-1,) + (1,) * (len(dims) - 1 - dim))
    return factor_of


def centred(stream_key, extent, deviation, limit, cuts=(), held_as=jnp.bfloat16):
    array = deviation * jax.random.normal(stream_key, extent, jnp.float32)
    if cuts:
        array = array * block_scale(stream_key, extent, cuts, -0.22, 0.18)
    return jnp.clip(array, -limit, limit).astype(held_as)


def heavy_noise(stream_key, dims, width, limit, shards, heavy, kind=jnp.bfloat16):
    values = width * jax.random.normal(stream_key, dims, jnp.float32)
    if shards:
        values = values * block_scale(stream_key, dims, shards, -0.22, 0.18)
    return jnp.clip(strengthened(values, jax.random.fold_in(stream_key, 3), *heavy), -limit, limit).astype(kind)


def setup_inputs(seed: int = 0) -> dict:
    key_of = jax.random.split(jax.random.key(seed), 5)
    primaries_start = centred(key_of[0], (NS, T_SIZE, S), 1.0, 6.0, ((0, 32),), jnp.float32)
    surface_operator = heavy_noise(key_of[1], (NF, 2, R, NS), (2 * NS) ** -0.5, 0.25, ((0, 8), (2, 4)), (2, 3, 4, 2.0))
    data_spectra = centred(key_of[2], (R, NF, 2, S), 1.0, 6.0, ((0, 4), (1, 8)))
    shrinkage = jnp.clip(jnp.exp(jax.random.uniform(key_of[3], (S,), jnp.float32, math.log(0.2), math.log(2.0))), 0.2, 2.0)
    return dict(primaries_start=primaries_start, surface_operator=surface_operator, data_spectra=data_spectra, shrinkage=shrinkage)


def transform_table(frequencies, samples):
    freq_index = jnp.arange(frequencies, dtype=jnp.int32)[:, None]
    sample_index = jnp.arange(samples, dtype=jnp.int32)[None, :]
    phase = freq_index * sample_index % samples
    angle = phase.astype(jnp.float32) * (2.0 * math.pi / samples)
    factor = math.sqrt(2.0 / samples)
    return jnp.stack([factor * jnp.cos(angle), -factor * jnp.sin(angle)], axis=1).astype(jnp.bfloat16)

def widen(values):
    return lax.optimization_barrier(values.astype(jnp.bfloat16)).astype(jnp.float32)

def one_frequency(items):
    operator, spectrum, recorded = items
    real_op = operator[0]
    imag_op = operator[1]
    real_in = spectrum[:, 0]
    imag_in = spectrum[:, 1]
    real_out = jnp.dot(real_op, real_in, preferred_element_type=jnp.float32) - jnp.dot(imag_op, imag_in, preferred_element_type=jnp.float32)
    imag_out = jnp.dot(real_op, imag_in, preferred_element_type=jnp.float32) + jnp.dot(imag_op, real_in, preferred_element_type=jnp.float32)
    resid = (recorded.astype(jnp.float32) - jnp.stack([real_out, imag_out], axis=1)).astype(jnp.bfloat16)
    real_res = resid[:, 0]
    imag_res = resid[:, 1]
    real_dir = jnp.dot(real_op.T, real_res, preferred_element_type=jnp.float32) + jnp.dot(imag_op.T, imag_res, preferred_element_type=jnp.float32)
    imag_dir = jnp.dot(real_op.T, imag_res, preferred_element_type=jnp.float32) - jnp.dot(imag_op.T, real_res, preferred_element_type=jnp.float32)
    return (resid, jnp.stack([real_dir, imag_dir], axis=1))

def reference(primaries_start, surface_operator, data_spectra, shrinkage):
    table = transform_table(NF, T_SIZE).astype(jnp.float32)
    primaries = primaries_start
    count_total = 2.0 * NF * NS * S
    residual = data_spectra
    for iteration in range(ITERS):
        spectra = jnp.einsum('kct,nts->nkcs', table, widen(primaries)).astype(jnp.bfloat16)
        residual_f, direction_f = lax.map(one_frequency, (surface_operator, jnp.moveaxis(spectra, 1, 0), jnp.moveaxis(data_spectra, 1, 0)))
        residual = jnp.moveaxis(residual_f, 0, 1)
        direction = jnp.moveaxis(direction_f, 0, 1)
        residual_norm = jnp.sum(jnp.square(residual.astype(jnp.float32)))
        direction_norm = jnp.sum(jnp.square(direction))
        step_size = 0.5 * residual_norm / (direction_norm + 1e-06)
        threshold = shrinkage[None, None, :] * (step_size * jnp.sqrt(direction_norm / count_total))
        update = jnp.einsum('kct,nkcs->nts', table, widen(direction))
        moved = primaries + step_size * update
        primaries = moved - jnp.clip(moved, -threshold, threshold)
    return (primaries, residual)
```

```python
import functools
import math

import jax
import jax.numpy as jnp
from jax import lax
from jax.experimental import pallas as pl
from jax.experimental.pallas import tpu as pltpu
from jax.sharding import PartitionSpec as P

ITERS = 2
CORES = 2
MESH = pl.DeviceIdType.MESH
VMEM_LIMIT = 48 * 1024 * 1024


def transform_table(frequencies, samples):
    freq_index = jnp.arange(frequencies, dtype=jnp.int32)[:, None]
    sample_index = jnp.arange(samples, dtype=jnp.int32)[None, :]
    phase = freq_index * sample_index % samples
    angle = phase.astype(jnp.float32) * (2.0 * math.pi / samples)
    factor = math.sqrt(2.0 / samples)
    return jnp.stack([factor * jnp.cos(angle), -factor * jnp.sin(angle)], axis=1).astype(
        jnp.bfloat16
    )


def place(groups):
    freq = lax.axis_index("freq")
    rcv = lax.axis_index("rcv")
    return freq, rcv // CORES, lax.rem(rcv, CORES)


def peers_of(freqs, offset, freq, core):
    step, flip = offset // CORES, offset % CORES
    to_freq = lax.rem(freq + step, freqs)
    from_freq = lax.rem(freq + freqs - step, freqs)
    other = lax.rem(core + flip, CORES)
    return to_freq, from_freq, other


def enter(freqs, groups, freq, group, core):
    barrier = pltpu.get_barrier_semaphore()
    for offset in range(1, freqs * CORES):
        to_freq, _, other = peers_of(freqs, offset, freq, core)
        pl.semaphore_signal(
            barrier, inc=1, device_id=(to_freq, group * CORES + other), device_id_type=MESH
        )
    for hop in range(1, groups):
        there = lax.rem(group + hop, groups)
        pl.semaphore_signal(
            barrier, inc=1, device_id=(freq, there * CORES + core), device_id_type=MESH
        )
    pl.semaphore_wait(barrier, freqs * CORES - 1 + groups - 1)


def spread_kernel(freqs, groups, with_operator, *refs):
    if with_operator:
        spec, oper, data, gathered, oper_out, data_out, *sems = refs
        send, recv, send_y, recv_y, local, swap_send, swap_recv = sems
    else:
        spec, gathered, send, recv, send_y, recv_y, local = refs
    freq, group, core = place(groups)
    count = freqs * CORES
    enter(freqs, groups, freq, group, core)

    def slot(source_freq, source_core, source_group=group):
        return (source_group * CORES + source_core) * freqs + source_freq

    def direct(offset):
        to_freq, _, other = peers_of(freqs, offset, freq, core)
        return pltpu.make_async_remote_copy(
            src_ref=spec.at[to_freq * CORES + other],
            dst_ref=gathered.at[slot(freq, core)],
            send_sem=send.at[offset],
            recv_sem=recv.at[offset],
            device_id=(to_freq, group * CORES + other),
            device_id_type=MESH,
        )

    def forward(offset, hop):
        _, from_freq, other = peers_of(freqs, offset, freq, core)
        there = lax.rem(group + hop, groups)
        place_of = slot(from_freq, other)
        source = spec.at[freq * CORES + core] if offset == 0 else gathered.at[place_of]
        return pltpu.make_async_remote_copy(
            src_ref=source,
            dst_ref=gathered.at[place_of],
            send_sem=send_y.at[(hop - 1) * count + offset],
            recv_sem=recv_y.at[(hop - 1) * count + offset],
            device_id=(freq, there * CORES + core),
            device_id_type=MESH,
        )

    order = list(range(1, count))
    for offset in order:
        direct(offset).start()
    own = pltpu.make_async_copy(
        spec.at[freq * CORES + core], gathered.at[slot(freq, core)], local.at[0]
    )
    own.start()
    for hop in range(1, groups):
        forward(0, hop).start()
    others = []
    if with_operator:
        sibling = 1 - core
        held = oper.shape[2]
        rows = pl.ds(pl.multiple_of(core * held, 16), held)
        kept = oper_out.shape[0]
        for number, (source, target, first) in enumerate(
            [
                (
                    oper.at[pl.ds(sibling * kept, kept)],
                    oper_out.at[:, :, rows, :],
                    oper.at[pl.ds(core * kept, kept)],
                ),
                (data.at[sibling], data_out.at[:, rows, :], data.at[core]),
            ]
        ):
            away = pltpu.make_async_remote_copy(
                src_ref=source,
                dst_ref=target,
                send_sem=swap_send.at[number],
                recv_sem=swap_recv.at[number],
                device_id=(freq, group * CORES + sibling),
                device_id_type=MESH,
            )
            away.start()
            here = pltpu.make_async_copy(first, target, local.at[1 + number])
            here.start()
            others += [away, here]
    for offset in order:
        direct(offset).wait_recv()
        for hop in range(1, groups):
            forward(offset, hop).start()
    own.wait()
    for offset in order:
        direct(offset).wait_send()
    for hop in range(1, groups):
        for offset in range(count):
            forward(offset, hop).wait()
    for copy in others:
        copy.wait()


def collect_kernel(freqs, groups, with_residual, *refs):
    if with_residual:
        part, resid, total, square, resid_out, landed, ready, mine, *sems = refs
        send, recv, send_y, recv_y, local, swap_send, swap_recv = sems
    else:
        part, total, square, landed, ready, mine, send, recv, send_y, recv_y, local = refs
    freq, group, core = place(groups)
    count = freqs * CORES
    rows = part.shape[1]
    enter(freqs, groups, freq, group, core)

    def slot(freq_of, core_of, group_of):
        return (group_of * CORES + core_of) * freqs + freq_of

    def across(offset, hop):
        to_freq, _, other = peers_of(freqs, offset, freq, core)
        there = lax.rem(group + hop, groups)
        number = (hop - 1) * count + offset
        return pltpu.make_async_remote_copy(
            src_ref=part.at[slot(to_freq, other, there)],
            dst_ref=landed.at[number],
            send_sem=send_y.at[number],
            recv_sem=recv_y.at[number],
            device_id=(freq, there * CORES + core),
            device_id_type=MESH,
        )

    def fetch(offset):
        to_freq, _, other = peers_of(freqs, offset, freq, core)
        return pltpu.make_async_copy(
            part.at[slot(to_freq, other, group)], mine.at[offset], local.at[offset]
        )

    def direct(offset):
        to_freq, _, other = peers_of(freqs, offset, freq, core)
        return pltpu.make_async_remote_copy(
            src_ref=ready.at[offset],
            dst_ref=total.at[freq * CORES + core],
            send_sem=send.at[offset],
            recv_sem=recv.at[offset],
            device_id=(to_freq, group * CORES + other),
            device_id_type=MESH,
        )

    order = list(range(count - 1, -1, -1))
    others = []
    for offset in order:
        for hop in range(1, groups):
            across(offset, hop).start()
        fetch(offset).start()
    if with_residual:
        sibling = 1 - core
        held = resid.shape[2]
        kept = resid.shape[1]
        rows_of = resid_out.shape[0] // CORES
        away = pltpu.make_async_remote_copy(
            src_ref=resid.at[sibling],
            dst_ref=resid_out.at[pl.ds(core * kept, kept)],
            send_sem=swap_send.at[0],
            recv_sem=swap_recv.at[0],
            device_id=(freq, group * CORES + sibling),
            device_id_type=MESH,
        )
        away.start()
        here = pltpu.make_async_copy(
            resid.at[core], resid_out.at[pl.ds(core * kept, kept)], local.at[count]
        )
        here.start()
        others = [away, here]
    square[...] = jnp.zeros_like(square)
    tile = min(rows, 128)
    for offset in order:
        fetch(offset).wait()
        for hop in range(1, groups):
            across(offset, hop).wait_recv()

        @pl.loop(0, rows // tile)
        def add(step):
            here = pl.ds(pl.multiple_of(step * tile, tile), tile)
            value = mine[offset, here, :].astype(jnp.float32)
            for hop in range(1, groups):
                value += landed[(hop - 1) * count + offset, here, :].astype(jnp.float32)
            ready[offset, here, :] = value.astype(jnp.bfloat16)
            square[...] += jnp.sum((value * value).reshape(tile // 8, 8, -1), axis=0)

        if offset:
            direct(offset).start()
    last = pltpu.make_async_copy(ready.at[0], total.at[freq * CORES + core], local.at[count + 1])
    last.start()
    last.wait()
    for offset in range(1, count):
        direct(offset).wait()
    for hop in range(1, groups):
        for offset in range(count):
            across(offset, hop).wait_send()
    for copy in others:
        copy.wait()


def spread(freqs, groups, ident, spectra, operator=None, data=None):
    count = freqs * CORES
    _, rows, width = spectra.shape
    shapes = [jax.ShapeDtypeStruct((groups * count, rows, width), jnp.bfloat16)]
    dma = pltpu.SemaphoreType.DMA
    sems = [dma((count,)), dma((count,)), dma(((groups - 1) * count,)), dma(((groups - 1) * count,)), dma((3,))]
    args = [spectra]
    if operator is not None:
        kb, two, held, points = operator.shape
        _, kept, _, width = data.shape
        shapes += [
            jax.ShapeDtypeStruct((kb // CORES, two, held * CORES, points), jnp.bfloat16),
            jax.ShapeDtypeStruct((kept, held * CORES, width), jnp.bfloat16),
        ]
        sems += [dma((2,)), dma((2,))]
        args += [operator, data]
    anywhere = pl.BlockSpec(memory_space=pl.ANY)
    return pl.pallas_call(
        functools.partial(spread_kernel, freqs, groups, operator is not None),
        out_shape=shapes,
        in_specs=[anywhere] * len(args),
        out_specs=[anywhere] * len(shapes),
        scratch_shapes=sems,
        compiler_params=pltpu.CompilerParams(
            collective_id=ident, has_side_effects=True, vmem_limit_bytes=VMEM_LIMIT
        ),
    )(*args)


def collect(freqs, groups, ident, part, resid=None):
    count = freqs * CORES
    _, rows, width = part.shape
    dma = pltpu.SemaphoreType.DMA
    shapes = [
        jax.ShapeDtypeStruct((count, rows, width), jnp.bfloat16),
        jax.ShapeDtypeStruct((8, width), jnp.float32),
    ]
    scratch = [
        pltpu.VMEM(((groups - 1) * count, rows, width), jnp.bfloat16),
        pltpu.VMEM((count, rows, width), jnp.bfloat16),
        pltpu.VMEM((count, rows, width), jnp.bfloat16),
        dma((count,)), dma((count,)), dma(((groups - 1) * count,)), dma(((groups - 1) * count,)), dma((count + 2,)),
    ]
    anywhere = pl.BlockSpec(memory_space=pl.ANY)
    outs = [anywhere, pl.BlockSpec(memory_space=pltpu.VMEM)]
    args = [part]
    if resid is not None:
        _, kept, held, _ = resid.shape
        shapes.append(jax.ShapeDtypeStruct((kept * CORES, held, width), jnp.bfloat16))
        outs.append(anywhere)
        scratch += [dma((1,)), dma((1,))]
        args.append(resid)
    return pl.pallas_call(
        functools.partial(collect_kernel, freqs, groups, resid is not None),
        out_shape=shapes,
        in_specs=[anywhere] * len(args),
        out_specs=outs,
        scratch_shapes=scratch,
        compiler_params=pltpu.CompilerParams(
            collective_id=ident, has_side_effects=True, vmem_limit_bytes=VMEM_LIMIT
        ),
    )(*args)


def local(freqs, groups, primaries_start, surface_operator, data_spectra, shrinkage):
    points, samples, sources = primaries_start.shape
    band, _, held, all_points = surface_operator.shape
    kept = band // CORES
    count = freqs * CORES
    everywhere = groups * count
    frequencies = band * freqs
    width = 2 * sources
    table = transform_table(frequencies, samples)
    primaries = primaries_start
    count_total = 2.0 * frequencies * all_points * sources

    data = data_spectra.reshape(held, CORES, kept, width).transpose(1, 2, 0, 3)
    operator = recorded = None
    for iteration in range(ITERS):
        local_spectra = jnp.einsum(
            "kct,nts->kncs",
            table,
            primaries.astype(jnp.bfloat16),
            preferred_element_type=jnp.float32,
        ).astype(jnp.bfloat16).reshape(count, kept * points, width)
        if iteration == 0:
            spectra, operator, recorded = spread(
                freqs, groups, 0, local_spectra, surface_operator, data
            )
        else:
            (spectra,) = spread(freqs, groups, 2, local_spectra)
        spectra = spectra.reshape(everywhere, kept, points, width).transpose(1, 0, 2, 3)
        spectra = spectra.reshape(kept, all_points, width)
        resid, direction = products(operator, spectra, recorded)
        residual_sq = jnp.sum(jnp.square(resid.astype(jnp.float32)))
        part = direction.reshape(kept, everywhere, points, width).transpose(1, 0, 2, 3)
        part = part.reshape(everywhere, kept * points, width)
        if iteration < ITERS - 1:
            total, square = collect(freqs, groups, 1, part)
        else:
            halves = resid.reshape(kept, CORES, held, width).transpose(1, 0, 2, 3)
            total, square, residual = collect(freqs, groups, 3, part, halves)
        residual_norm, direction_norm = lax.psum(
            (residual_sq, jnp.sum(square)), ("freq", "rcv")
        )
        step_size = 0.5 * residual_norm / (direction_norm + 1e-06)
        threshold = shrinkage[None, None, :] * (step_size * jnp.sqrt(direction_norm / count_total))
        update = jnp.einsum(
            "kct,kncs->nts",
            table,
            total.reshape(frequencies, points, 2, sources),
            preferred_element_type=jnp.float32,
        )
        moved = primaries + step_size * update
        primaries = moved - jnp.clip(moved, -threshold, threshold)
    residual = residual.transpose(1, 0, 2).reshape(held, band, 2, sources)
    return (primaries, residual)


def products(operator, spectra, recorded):
    sources = spectra.shape[2] // 2
    real_op, imag_op = operator[:, 0], operator[:, 1]

    def turned(values, sign):
        return jnp.concatenate(
            [-sign * values[:, :, sources:], sign * values[:, :, :sources]], axis=2
        )

    def product(left, right, order):
        return jnp.einsum(order, left, right, preferred_element_type=jnp.float32)

    ahead = "krn,kns->krs"
    back = "krn,krs->kns"
    predicted = product(real_op, spectra, ahead) + product(imag_op, turned(spectra, 1), ahead)
    resid = (recorded.astype(jnp.float32) - predicted).astype(jnp.bfloat16)
    direction = product(real_op, resid, back) + product(imag_op, turned(resid, -1), back)
    return resid, direction.astype(jnp.bfloat16)


def solution(mesh):
    freqs = mesh.shape["freq"]
    groups = mesh.shape["rcv"] // CORES
    return jax.shard_map(
        functools.partial(local, freqs, groups),
        mesh=mesh,
        in_specs=(
            P(("rcv", "freq"), None, None),
            P("freq", None, "rcv", None),
            P("rcv", "freq", None, None),
            P(),
        ),
        out_specs=(P(("rcv", "freq"), None, None), P("rcv", "freq", None, None)),
        check_vma=False,
    )
```

```python
import functools
import math

import jax
import jax.numpy as jnp
import numpy as np
from jax import lax
from jax.experimental import pallas as pl
from jax.experimental.pallas import tpu as pltpu
from jax.sharding import PartitionSpec as P

ITERS = 2
CORES = 2
SWAPS = 8
MESH = pl.DeviceIdType.MESH
VMEM_LIMIT = 56 * 1024 * 1024


def transform_table(frequencies, samples):
    phase = np.arange(frequencies)[:, None] * np.arange(samples)[None, :] % samples
    angle = phase * (2.0 * math.pi / samples)
    factor = math.sqrt(2.0 / samples)
    rows = np.concatenate([factor * np.cos(angle), -factor * np.sin(angle)], axis=0)
    return rows.astype(np.float32).astype(jnp.bfloat16)


def place(groups):
    freq = lax.axis_index("freq")
    rcv = lax.axis_index("rcv")
    return freq, rcv // CORES, lax.rem(rcv, CORES)


def peers_of(freqs, offset, freq, core):
    step, flip = offset // CORES, offset % CORES
    to_freq = lax.rem(freq + step, freqs)
    from_freq = lax.rem(freq + freqs - step, freqs)
    other = lax.rem(core + flip, CORES)
    return to_freq, from_freq, other


def enter(freqs, groups, freq, group, core):
    barrier = pltpu.get_barrier_semaphore()
    for offset in range(1, freqs * CORES):
        to_freq, _, other = peers_of(freqs, offset, freq, core)
        pl.semaphore_signal(
            barrier, inc=1, device_id=(to_freq, group * CORES + other), device_id_type=MESH
        )
    for hop in range(1, groups):
        there = lax.rem(group + hop, groups)
        pl.semaphore_signal(
            barrier, inc=1, device_id=(freq, there * CORES + core), device_id_type=MESH
        )
    pl.semaphore_wait(barrier, freqs * CORES - 1 + groups - 1)


def spread_kernel(freqs, groups, with_operator, *refs):
    if with_operator:
        spec, oper, data, gathered, oper_out, data_out, *sems = refs
        send, recv, send_y, recv_y, local, swap_send, swap_recv = sems
    else:
        spec, gathered, send, recv, send_y, recv_y, local = refs
    freq, group, core = place(groups)
    count = freqs * CORES
    enter(freqs, groups, freq, group, core)

    def slot(source_freq, source_core, source_group=group):
        return (source_group * CORES + source_core) * freqs + source_freq

    def direct(offset):
        to_freq, _, other = peers_of(freqs, offset, freq, core)
        return pltpu.make_async_remote_copy(
            src_ref=spec.at[to_freq * CORES + other],
            dst_ref=gathered.at[slot(freq, core)],
            send_sem=send.at[offset],
            recv_sem=recv.at[offset],
            device_id=(to_freq, group * CORES + other),
            device_id_type=MESH,
        )

    def forward(offset, hop):
        _, from_freq, other = peers_of(freqs, offset, freq, core)
        there = lax.rem(group + hop, groups)
        place_of = slot(from_freq, other)
        source = spec.at[freq * CORES + core] if offset == 0 else gathered.at[place_of]
        return pltpu.make_async_remote_copy(
            src_ref=source,
            dst_ref=gathered.at[place_of],
            send_sem=send_y.at[(hop - 1) * count + offset],
            recv_sem=recv_y.at[(hop - 1) * count + offset],
            device_id=(freq, there * CORES + core),
            device_id_type=MESH,
        )

    order = list(range(1, count))
    for offset in order:
        direct(offset).start()
    own = pltpu.make_async_copy(
        spec.at[freq * CORES + core], gathered.at[slot(freq, core)], local.at[0]
    )
    own.start()
    for hop in range(1, groups):
        forward(0, hop).start()
    others = []
    if with_operator:
        sibling = 1 - core
        kept = oper_out.shape[0]
        size = kept // SWAPS
        pieces = [(data.at[sibling], data_out)]
        for piece in range(SWAPS):
            pieces.append(
                (
                    oper.at[pl.ds(sibling * kept + piece * size, size)],
                    oper_out.at[pl.ds(piece * size, size)],
                )
            )
        for number, (source, target) in enumerate(pieces):
            away = pltpu.make_async_remote_copy(
                src_ref=source,
                dst_ref=target,
                send_sem=swap_send.at[number],
                recv_sem=swap_recv.at[number],
                device_id=(freq, group * CORES + sibling),
                device_id_type=MESH,
            )
            away.start()
            others.append(away)
    for offset in order:
        direct(offset).wait_recv()
        for hop in range(1, groups):
            forward(offset, hop).start()
    own.wait()
    for offset in order:
        direct(offset).wait_send()
    for hop in range(1, groups):
        for offset in range(count):
            forward(offset, hop).wait()
    for copy in others:
        copy.wait()


def collect_kernel(freqs, groups, with_residual, *refs):
    if with_residual:
        part, resid_sq, resid, resid_away, total, norms, resid_out, *rest = refs
        *rest, swap_send, swap_recv = rest
    else:
        part, resid_sq, total, norms, *rest = refs
    landed, ready, mine, sums, sums_y, sums_all, *rest = rest
    send, recv, send_y, recv_y, local, norm_send, norm_recv = rest
    freq, group, core = place(groups)
    count = freqs * CORES
    rows = part.shape[1]
    enter(freqs, groups, freq, group, core)

    def slot(freq_of, core_of, group_of):
        return (group_of * CORES + core_of) * freqs + freq_of

    def across(offset, hop):
        to_freq, _, other = peers_of(freqs, offset, freq, core)
        there = lax.rem(group + hop, groups)
        number = (hop - 1) * count + offset
        return pltpu.make_async_remote_copy(
            src_ref=part.at[slot(to_freq, other, there)],
            dst_ref=landed.at[number],
            send_sem=send_y.at[number],
            recv_sem=recv_y.at[number],
            device_id=(freq, there * CORES + core),
            device_id_type=MESH,
        )

    def fetch(offset):
        to_freq, _, other = peers_of(freqs, offset, freq, core)
        return pltpu.make_async_copy(
            part.at[slot(to_freq, other, group)], mine.at[offset], local.at[offset]
        )

    def direct(offset):
        to_freq, _, other = peers_of(freqs, offset, freq, core)
        return pltpu.make_async_remote_copy(
            src_ref=ready.at[offset],
            dst_ref=total.at[freq * CORES + core],
            send_sem=send.at[offset],
            recv_sem=recv.at[offset],
            device_id=(to_freq, group * CORES + other),
            device_id_type=MESH,
        )

    order = list(range(count - 1, -1, -1))
    others = []
    for offset in order:
        for hop in range(1, groups):
            across(offset, hop).start()
        fetch(offset).start()
    if with_residual:
        sibling = 1 - core
        kept = resid.shape[0]
        away = pltpu.make_async_remote_copy(
            src_ref=resid_away,
            dst_ref=resid_out.at[pl.ds(core * kept, kept)],
            send_sem=swap_send.at[0],
            recv_sem=swap_recv.at[0],
            device_id=(freq, group * CORES + sibling),
            device_id_type=MESH,
        )
        away.start()
        here = pltpu.make_async_copy(
            resid, resid_out.at[pl.ds(core * kept, kept)], local.at[count]
        )
        here.start()
        others = [away, here]
    sums[0] = resid_sq[...]
    sums[1] = jnp.zeros_like(resid_sq)
    tile = min(rows, 128)
    for offset in order:
        fetch(offset).wait()
        for hop in range(1, groups):
            across(offset, hop).wait_recv()

        @pl.loop(0, rows // tile)
        def add(step):
            here = pl.ds(pl.multiple_of(step * tile, tile), tile)
            value = mine[offset, here, :].astype(jnp.float32)
            for hop in range(1, groups):
                value += landed[(hop - 1) * count + offset, here, :].astype(jnp.float32)
            ready[offset, here, :] = value.astype(jnp.bfloat16)
            sums[1] += jnp.sum((value * value).reshape(tile // 8, 8, -1), axis=0)

        if offset:
            direct(offset).start()
    def norm_across(hop):
        there = lax.rem(group + hop, groups)
        return pltpu.make_async_remote_copy(
            src_ref=sums,
            dst_ref=sums_y.at[hop - 1],
            send_sem=norm_send.at[count + hop - 1],
            recv_sem=norm_recv.at[count + hop - 1],
            device_id=(freq, there * CORES + core),
            device_id_type=MESH,
        )

    def norm_direct(offset):
        to_freq, _, other = peers_of(freqs, offset, freq, core)
        return pltpu.make_async_remote_copy(
            src_ref=sums_all.at[0],
            dst_ref=sums_all.at[offset],
            send_sem=norm_send.at[offset],
            recv_sem=norm_recv.at[offset],
            device_id=(to_freq, group * CORES + other),
            device_id_type=MESH,
        )

    for hop in range(1, groups):
        norm_across(hop).start()
    last = pltpu.make_async_copy(ready.at[0], total.at[freq * CORES + core], local.at[count + 1])
    last.start()
    value = sums[...]
    for hop in range(1, groups):
        norm_across(hop).wait()
        value = value + sums_y[hop - 1]
    sums_all[0] = value
    for offset in range(1, count):
        norm_direct(offset).start()
    for offset in range(1, count):
        norm_direct(offset).wait()
        value = value + sums_all[offset]
    norms[...] = value
    last.wait()
    for offset in range(1, count):
        direct(offset).wait()
    for hop in range(1, groups):
        for offset in range(count):
            across(offset, hop).wait_send()
    for copy in others:
        copy.wait()


def spread(freqs, groups, ident, spectra, operator=None, data=None):
    count = freqs * CORES
    _, rows, width = spectra.shape
    shapes = [jax.ShapeDtypeStruct((groups * count, rows, width), jnp.bfloat16)]
    dma = pltpu.SemaphoreType.DMA
    sems = [dma((count,)), dma((count,)), dma(((groups - 1) * count,)), dma(((groups - 1) * count,)), dma((3,))]
    args = [spectra]
    if operator is not None:
        kb, two, held, points = operator.shape
        _, kept, _, width = data.shape
        shapes += [
            jax.ShapeDtypeStruct((kb // CORES, two, held, points), jnp.bfloat16),
            jax.ShapeDtypeStruct((kept, held, width), jnp.bfloat16),
        ]
        sems += [dma((SWAPS + 1,)), dma((SWAPS + 1,))]
        args += [operator, data]
    anywhere = pl.BlockSpec(memory_space=pl.ANY)
    return pl.pallas_call(
        functools.partial(spread_kernel, freqs, groups, operator is not None),
        out_shape=shapes,
        in_specs=[anywhere] * len(args),
        out_specs=[anywhere] * len(shapes),
        scratch_shapes=sems,
        compiler_params=pltpu.CompilerParams(
            collective_id=ident, has_side_effects=True, vmem_limit_bytes=VMEM_LIMIT
        ),
    )(*args)


def collect(freqs, groups, ident, part, resid_sq, resid=None, resid_away=None):
    count = freqs * CORES
    _, rows, width = part.shape
    dma = pltpu.SemaphoreType.DMA
    pair = (2,) + resid_sq.shape
    shapes = [
        jax.ShapeDtypeStruct((count, rows, width), jnp.bfloat16),
        jax.ShapeDtypeStruct(pair, jnp.float32),
    ]
    scratch = [
        pltpu.VMEM(((groups - 1) * count, rows, width), jnp.bfloat16),
        pltpu.VMEM((count, rows, width), jnp.bfloat16),
        pltpu.VMEM((count, rows, width), jnp.bfloat16),
        pltpu.VMEM(pair, jnp.float32),
        pltpu.VMEM((groups - 1,) + pair, jnp.float32),
        pltpu.VMEM((count,) + pair, jnp.float32),
        dma((count,)), dma((count,)), dma(((groups - 1) * count,)), dma(((groups - 1) * count,)), dma((count + 2,)),
        dma((count + groups - 1,)), dma((count + groups - 1,)),
    ]
    anywhere = pl.BlockSpec(memory_space=pl.ANY)
    outs = [anywhere, pl.BlockSpec(memory_space=pltpu.VMEM)]
    args = [part, resid_sq]
    if resid is not None:
        kept, held, _ = resid.shape
        shapes.append(jax.ShapeDtypeStruct((kept * CORES, held, width), jnp.bfloat16))
        outs.append(anywhere)
        scratch += [dma((1,)), dma((1,))]
        args += [resid, resid_away]
    return pl.pallas_call(
        functools.partial(collect_kernel, freqs, groups, resid is not None),
        out_shape=shapes,
        in_specs=[anywhere, pl.BlockSpec(memory_space=pltpu.VMEM)] + [anywhere] * (len(args) - 2),
        out_specs=outs,
        scratch_shapes=scratch,
        compiler_params=pltpu.CompilerParams(
            collective_id=ident, has_side_effects=True, vmem_limit_bytes=VMEM_LIMIT
        ),
    )(*args)


def interleave(value, scratch, point, sources, frequencies):
    stride = scratch[0].shape[0] // frequencies
    for which in range(2):
        for part in range(2):
            scratch[part][pl.ds(point + which, frequencies, stride=stride), :] = value[
                part * frequencies : (part + 1) * frequencies,
                which * sources : (which + 1) * sources,
            ]


def write_out(out, scratch, sources):
    tile = 1024

    @pl.loop(0, out.shape[0] // tile)
    def write(step):
        rows = pl.ds(pl.multiple_of(step * tile, tile), tile)
        for part in range(2):
            out[rows, part * sources : (part + 1) * sources] = scratch[part][rows, :].astype(
                jnp.bfloat16
            )


def pair_of(prim):
    return jnp.concatenate([prim[0], prim[1]], axis=1)


def forward_kernel(prim, table, out, *scratch):
    sources = prim.shape[2]
    frequencies = table.shape[0] // 2
    step = pl.program_id(0)
    value = jnp.dot(
        table[...], pair_of(prim).astype(jnp.bfloat16), preferred_element_type=jnp.float32
    )
    interleave(value, scratch, 2 * step, sources, frequencies)

    @pl.when(step == pl.num_programs(0) - 1)
    def finish():
        write_out(out, scratch, sources)


def update_kernel(count_total, last, *refs):
    if last:
        norms, shrink, total, prim, turned_table, prim_out, real, imag = refs
    else:
        norms, shrink, total, prim, turned_table, table, prim_out, out, real, imag, *scratch = refs
    sources = prim.shape[2]
    frequencies = turned_table.shape[1] // 2
    stride = total.shape[0] // frequencies
    step = pl.program_id(0)
    tile = 1024

    @pl.when(step == 0)
    def widen():
        @pl.loop(0, total.shape[0] // tile)
        def copy(step):
            rows = pl.ds(pl.multiple_of(step * tile, tile), tile)
            real[rows, :] = total[rows, :sources].astype(jnp.float32)
            imag[rows, :] = total[rows, sources:].astype(jnp.float32)

    residual_norm = jnp.sum(norms[0], axis=(0, 1), keepdims=True)
    direction_norm = jnp.sum(norms[1], axis=(0, 1), keepdims=True)
    step_size = 0.5 * residual_norm / (direction_norm + 1e-06)
    threshold = shrink[...] * (step_size * jnp.sqrt(direction_norm / count_total))
    threshold = jnp.concatenate([threshold, threshold], axis=1)

    def column(point):
        rows = pl.ds(point, frequencies, stride=stride)
        return jnp.concatenate([real[rows, :], imag[rows, :]], axis=0).astype(jnp.bfloat16)

    both = jnp.concatenate([column(2 * step), column(2 * step + 1)], axis=1)
    update = jnp.dot(turned_table[...], both, preferred_element_type=jnp.float32)
    moved = pair_of(prim) + step_size * update
    fresh = moved - jnp.clip(moved, -threshold, threshold)
    prim_out[0] = fresh[:, :sources]
    prim_out[1] = fresh[:, sources:]
    if last:
        return
    value = jnp.dot(table[...], fresh.astype(jnp.bfloat16), preferred_element_type=jnp.float32)
    interleave(value, scratch, 2 * step, sources, frequencies)

    @pl.when(step == pl.num_programs(0) - 1)
    def finish():
        write_out(out, scratch, sources)


def products_kernel(core_ref, near, far, spectra, near_data, far_data, near_res, far_res, part, square):
    held = near.shape[2]
    points = spectra.shape[0] * spectra.shape[2]
    width = spectra.shape[3]
    sources = width // 2
    values = spectra[...].reshape(points, width)
    real_op = jnp.concatenate([near[0, 0], far[0, 0]], axis=0)
    imag_op = jnp.concatenate([near[0, 1], far[0, 1]], axis=0)

    def product(left, right, side):
        return lax.dot_general(
            left, right, (((side,), (0,)), ((), ())), preferred_element_type=jnp.float32
        )

    def turned(values):
        return jnp.concatenate([-values[:, sources:], values[:, :sources]], axis=1)

    predicted = product(real_op, values, 1) + product(imag_op, turned(values), 1)
    recorded = jnp.concatenate([near_data[0, 0], far_data[0]], axis=0).astype(jnp.float32)
    resid = (recorded - predicted).astype(jnp.bfloat16)
    near_res[0] = resid[:held]
    far_res[0] = resid[held:]

    @pl.when(pl.program_id(0) == 0)
    def clear():
        square[...] = jnp.zeros_like(square)

    wide = resid.astype(jnp.float32)
    square[...] += jnp.sum((wide * wide).reshape(-1, 8, width), axis=0)
    direction = product(real_op, resid, 0) - product(imag_op, turned(resid), 0)
    part[...] = direction.astype(jnp.bfloat16).reshape(part.shape)


def params():
    return pltpu.CompilerParams(vmem_limit_bytes=VMEM_LIMIT)


def once(shape):
    return pl.BlockSpec(shape, lambda *_: (0,) * len(shape), pipeline_mode=pl.Buffered(1))


def forward(prim, table):
    points, samples, sources = prim.shape
    rows = table.shape[0] // 2 * points
    return pl.pallas_call(
        forward_kernel,
        grid=(points // 2,),
        out_shape=jax.ShapeDtypeStruct((rows, 2 * sources), jnp.bfloat16),
        in_specs=[pl.BlockSpec((2, samples, sources), lambda i: (i, 0, 0)), once(table.shape)],
        out_specs=once((rows, 2 * sources)),
        scratch_shapes=[pltpu.VMEM((rows, sources), jnp.float32)] * 2,
        compiler_params=params(),
    )(prim, table)


def advance(norms, shrink, total, prim, turned_table, table, count_total, last):
    points, samples, sources = prim.shape
    rows = total.shape[0]
    block = pl.BlockSpec((2, samples, sources), lambda i: (i, 0, 0))
    args = [norms, shrink, total, prim, turned_table]
    specs = [once(norms.shape), once(shrink.shape), once(total.shape), block, once(turned_table.shape)]
    shapes, outs = [jax.ShapeDtypeStruct(prim.shape, jnp.float32)], [block]
    scratch = [pltpu.VMEM((rows, sources), jnp.float32)] * (2 if last else 4)
    if not last:
        args.append(table)
        specs.append(once(table.shape))
        shapes.append(jax.ShapeDtypeStruct(total.shape, jnp.bfloat16))
        outs.append(once(total.shape))
    return pl.pallas_call(
        functools.partial(update_kernel, count_total, last),
        grid=(points // 2,),
        out_shape=shapes,
        in_specs=specs,
        out_specs=outs,
        scratch_shapes=scratch,
        compiler_params=params(),
    )(*args)


def products(core, near, far, spectra, near_data, far_data):
    kept, _, held, _ = far.shape
    everywhere, _, points, width = spectra.shape
    rows = pl.BlockSpec((1, held, width), lambda k, c: (k, 0, 0))
    spread_block = pl.BlockSpec((everywhere, 1, points, width), lambda k, c: (0, k, 0, 0))
    resid_shape = jax.ShapeDtypeStruct((kept, held, width), jnp.bfloat16)
    return pl.pallas_call(
        products_kernel,
        grid_spec=pltpu.PrefetchScalarGridSpec(
            num_scalar_prefetch=1,
            grid=(kept,),
            in_specs=[
                pl.BlockSpec((1,) + far.shape[1:], lambda k, c: (c[0] * kept + k, 0, 0, 0)),
                pl.BlockSpec((1,) + far.shape[1:], lambda k, c: (k, 0, 0, 0)),
                spread_block,
                pl.BlockSpec((1, 1, held, width), lambda k, c: (c[0], k, 0, 0)),
                rows,
            ],
            out_specs=[rows, rows, spread_block, pl.BlockSpec((8, width), lambda k, c: (0, 0))],
        ),
        out_shape=[
            resid_shape,
            resid_shape,
            jax.ShapeDtypeStruct(spectra.shape, jnp.bfloat16),
            jax.ShapeDtypeStruct((8, width), jnp.float32),
        ],
        compiler_params=params(),
    )(core, near, far, spectra, near_data, far_data)


def plain_forward(prim, table):
    points, samples, sources = prim.shape
    spectra = jnp.einsum(
        "ckt,nts->kncs",
        table.reshape(2, -1, samples),
        prim.astype(jnp.bfloat16),
        preferred_element_type=jnp.float32,
    ).astype(jnp.bfloat16)
    return spectra.reshape(-1, 2 * sources)


def plain_advance(norms, shrink, total, prim, turned_table, table, count_total, last):
    points, samples, sources = prim.shape
    residual_norm, direction_norm = jnp.sum(norms[0]), jnp.sum(norms[1])
    step_size = 0.5 * residual_norm / (direction_norm + 1e-06)
    threshold = shrink[:, None, :] * (step_size * jnp.sqrt(direction_norm / count_total))
    update = jnp.einsum(
        "ckt,kncs->nts",
        table.reshape(2, -1, samples),
        total.reshape(-1, points, 2, sources),
        preferred_element_type=jnp.float32,
    )
    moved = prim + step_size * update
    fresh = moved - jnp.clip(moved, -threshold, threshold)
    return (fresh,) if last else (fresh, plain_forward(fresh, table))


def plain_products(core, near, far, spectra, near_data, far_data):
    kept, _, held, _ = far.shape
    everywhere, _, points, width = spectra.shape
    sources = width // 2
    near = lax.dynamic_slice_in_dim(near, core[0] * kept, kept, 0)
    operator = jnp.concatenate([near, far], axis=2)
    near_data = lax.dynamic_index_in_dim(near_data, core[0], 0, keepdims=False)
    recorded = jnp.concatenate([near_data, far_data], axis=1)
    values = spectra.transpose(1, 0, 2, 3).reshape(kept, everywhere * points, width)

    def turned(values):
        return jnp.concatenate([-values[:, :, sources:], values[:, :, :sources]], axis=2)

    def product(order, part, right):
        return jnp.einsum(order, operator[:, part], right, preferred_element_type=jnp.float32)

    ahead, back = "krn,kns->krs", "krn,krs->kns"
    predicted = product(ahead, 0, values) + product(ahead, 1, turned(values))
    resid = (recorded.astype(jnp.float32) - predicted).astype(jnp.bfloat16)
    square = jnp.sum(jnp.square(resid.astype(jnp.float32)).reshape(-1, 8, width), axis=0)
    direction = product(back, 0, resid) - product(back, 1, turned(resid))
    part = direction.astype(jnp.bfloat16).reshape(kept, everywhere, points, width)
    return resid[:, :held], resid[:, held:], part.transpose(1, 0, 2, 3), square


def local(freqs, groups, primaries_start, surface_operator, data_spectra, shrinkage):
    points, samples, sources = primaries_start.shape
    band, _, held, all_points = surface_operator.shape
    kept = band // CORES
    count = freqs * CORES
    everywhere = groups * count
    frequencies = band * freqs
    width = 2 * sources
    rows = transform_table(frequencies, samples)
    table, turned_table = jnp.asarray(rows), jnp.asarray(np.ascontiguousarray(rows.T))
    primaries = primaries_start
    count_total = 2.0 * frequencies * all_points * sources
    whole_tiles = points % 16 == 0
    go_forward, go_advance, multiply = (
        (forward, advance, products)
        if whole_tiles
        else (plain_forward, plain_advance, plain_products)
    )

    core = lax.rem(lax.axis_index("rcv"), CORES).astype(jnp.int32).reshape(1)
    data = data_spectra.reshape(held, CORES, kept, width).transpose(1, 2, 0, 3)
    shrink = shrinkage.reshape(1, sources)
    local_spectra = go_forward(primaries, table)
    for iteration in range(ITERS):
        last = iteration == ITERS - 1
        message = local_spectra.reshape(count, kept * points, width)
        if iteration == 0:
            spectra, far, far_data = spread(freqs, groups, 0, message, surface_operator, data)
        else:
            (spectra,) = spread(freqs, groups, 2, message)
        near_res, far_res, part, square = multiply(
            core,
            surface_operator,
            far,
            spectra.reshape(everywhere, kept, points, width),
            data,
            far_data,
        )
        part = part.reshape(everywhere, kept * points, width)
        if not last:
            total, norms = collect(freqs, groups, 1, part, square)
        else:
            total, norms, residual = collect(freqs, groups, 3, part, square, near_res, far_res)
        total = total.reshape(frequencies * points, width)
        primaries, *more = go_advance(
            norms, shrink, total, primaries, turned_table, table, count_total, last
        )
        if more:
            (local_spectra,) = more
    residual = residual.transpose(1, 0, 2).reshape(held, band, 2, sources)
    return (primaries, residual)


def solution(mesh):
    freqs = mesh.shape["freq"]
    groups = mesh.shape["rcv"] // CORES
    return jax.shard_map(
        functools.partial(local, freqs, groups),
        mesh=mesh,
        in_specs=(
            P(("rcv", "freq"), None, None),
            P("freq", None, "rcv", None),
            P("rcv", "freq", None, None),
            P(),
        ),
        out_specs=(P(("rcv", "freq"), None, None), P("rcv", "freq", None, None)),
        check_vma=False,
    )
```

```python
import functools
import math

import jax
import jax.numpy as jnp
import numpy as np
from jax import lax
from jax.experimental import pallas as pl
from jax.experimental.pallas import tpu as pltpu
from jax.sharding import PartitionSpec as P

ITERS = 2
CORES = 2
SWAPS = 8
MESH = pl.DeviceIdType.MESH
VMEM_LIMIT = 56 * 1024 * 1024


def transform_table(frequencies, samples):
    phase = np.arange(frequencies)[:, None] * np.arange(samples)[None, :] % samples
    angle = phase * (2.0 * math.pi / samples)
    factor = math.sqrt(2.0 / samples)
    rows = np.concatenate([factor * np.cos(angle), -factor * np.sin(angle)], axis=0)
    return rows.astype(np.float32).astype(jnp.bfloat16)


def place(groups):
    freq = lax.axis_index("freq")
    rcv = lax.axis_index("rcv")
    return freq, rcv // CORES, lax.rem(rcv, CORES)


def peers_of(freqs, offset, freq, core):
    step, flip = offset // CORES, offset % CORES
    to_freq = lax.rem(freq + step, freqs)
    from_freq = lax.rem(freq + freqs - step, freqs)
    other = lax.rem(core + flip, CORES)
    return to_freq, from_freq, other


def far_first(freqs):
    steps = sorted(range(freqs), key=lambda step: (abs(step - freqs // 2), step))
    return [step * CORES + flip for step in steps for flip in range(CORES - 1, -1, -1)]


def mixed(freqs):
    steps = sorted(range(1, freqs), key=lambda step: (abs(step - freqs // 2), step))
    turn = []
    while steps:
        turn.append(steps.pop(0))
        if steps:
            turn.append(steps.pop(-1))
    return [1] + [step * CORES + flip for step in turn for flip in range(CORES)]


def enter(freqs, groups, freq, group, core):
    barrier = pltpu.get_barrier_semaphore()
    for offset in range(1, freqs * CORES):
        to_freq, _, other = peers_of(freqs, offset, freq, core)
        pl.semaphore_signal(
            barrier, inc=1, device_id=(to_freq, group * CORES + other), device_id_type=MESH
        )
    for hop in range(1, groups):
        there = lax.rem(group + hop, groups)
        pl.semaphore_signal(
            barrier, inc=1, device_id=(freq, there * CORES + core), device_id_type=MESH
        )
    pl.semaphore_wait(barrier, freqs * CORES - 1 + groups - 1)


def spread_kernel(freqs, groups, with_operator, *refs):
    if with_operator:
        spec, oper, data, gathered, oper_out, data_out, *sems = refs
        send, recv, send_y, recv_y, local, swap_send, swap_recv = sems
    else:
        spec, gathered, send, recv, send_y, recv_y, local = refs
    freq, group, core = place(groups)
    count = freqs * CORES
    enter(freqs, groups, freq, group, core)

    def slot(source_freq, source_core, source_group=group):
        return (source_group * CORES + source_core) * freqs + source_freq

    def direct(offset):
        to_freq, _, other = peers_of(freqs, offset, freq, core)
        return pltpu.make_async_remote_copy(
            src_ref=spec.at[to_freq * CORES + other],
            dst_ref=gathered.at[slot(freq, core)],
            send_sem=send.at[offset],
            recv_sem=recv.at[offset],
            device_id=(to_freq, group * CORES + other),
            device_id_type=MESH,
        )

    def forward(offset, hop):
        _, from_freq, other = peers_of(freqs, offset, freq, core)
        there = lax.rem(group + hop, groups)
        place_of = slot(from_freq, other)
        source = spec.at[freq * CORES + core] if offset == 0 else gathered.at[place_of]
        return pltpu.make_async_remote_copy(
            src_ref=source,
            dst_ref=gathered.at[place_of],
            send_sem=send_y.at[(hop - 1) * count + offset],
            recv_sem=recv_y.at[(hop - 1) * count + offset],
            device_id=(freq, there * CORES + core),
            device_id_type=MESH,
        )

    order = mixed(freqs)
    for offset in order:
        direct(offset).start()
    own = pltpu.make_async_copy(
        spec.at[freq * CORES + core], gathered.at[slot(freq, core)], local.at[0]
    )
    own.start()
    for hop in range(1, groups):
        forward(0, hop).start()
    others = []
    if with_operator:
        sibling = 1 - core
        kept = oper_out.shape[0]
        size = kept // SWAPS
        pieces = [(data.at[sibling], data_out)]
        for piece in range(SWAPS):
            pieces.append(
                (
                    oper.at[pl.ds(sibling * kept + piece * size, size)],
                    oper_out.at[pl.ds(piece * size, size)],
                )
            )
        for number, (source, target) in enumerate(pieces):
            away = pltpu.make_async_remote_copy(
                src_ref=source,
                dst_ref=target,
                send_sem=swap_send.at[number],
                recv_sem=swap_recv.at[number],
                device_id=(freq, group * CORES + sibling),
                device_id_type=MESH,
            )
            away.start()
            others.append(away)
    for offset in order:
        direct(offset).wait_recv()
        for hop in range(1, groups):
            forward(offset, hop).start()
    own.wait()
    for offset in order:
        direct(offset).wait_send()
    for hop in range(1, groups):
        for offset in range(count):
            forward(offset, hop).wait()
    for copy in others:
        copy.wait()


def collect_kernel(freqs, groups, with_residual, *refs):
    if with_residual:
        part, resid_sq, resid, resid_away, total, norms, resid_out, *rest = refs
        *rest, swap_send, swap_recv = rest
    else:
        part, resid_sq, total, norms, *rest = refs
    landed, ready, mine, sums, small, sums_y, sums_all, *rest = rest
    send, recv, send_y, recv_y, local, norm_send, norm_recv = rest
    freq, group, core = place(groups)
    count = freqs * CORES
    rows = part.shape[1]
    enter(freqs, groups, freq, group, core)

    def slot(freq_of, core_of, group_of):
        return (group_of * CORES + core_of) * freqs + freq_of

    def across(offset, hop):
        to_freq, _, other = peers_of(freqs, offset, freq, core)
        there = lax.rem(group + hop, groups)
        number = (hop - 1) * count + offset
        return pltpu.make_async_remote_copy(
            src_ref=part.at[slot(to_freq, other, there)],
            dst_ref=landed.at[number],
            send_sem=send_y.at[number],
            recv_sem=recv_y.at[number],
            device_id=(freq, there * CORES + core),
            device_id_type=MESH,
        )

    def fetch(offset):
        to_freq, _, other = peers_of(freqs, offset, freq, core)
        return pltpu.make_async_copy(
            part.at[slot(to_freq, other, group)], mine.at[offset], local.at[offset]
        )

    def direct(offset):
        to_freq, _, other = peers_of(freqs, offset, freq, core)
        return pltpu.make_async_remote_copy(
            src_ref=ready.at[offset],
            dst_ref=total.at[freq * CORES + core],
            send_sem=send.at[offset],
            recv_sem=recv.at[offset],
            device_id=(to_freq, group * CORES + other),
            device_id_type=MESH,
        )

    order = far_first(freqs)
    others = []
    for offset in order:
        for hop in range(1, groups):
            across(offset, hop).start()
        fetch(offset).start()
    if with_residual:
        sibling = 1 - core
        kept = resid.shape[0]
        away = pltpu.make_async_remote_copy(
            src_ref=resid_away,
            dst_ref=resid_out.at[pl.ds(core * kept, kept)],
            send_sem=swap_send.at[0],
            recv_sem=swap_recv.at[0],
            device_id=(freq, group * CORES + sibling),
            device_id_type=MESH,
        )
        away.start()
        here = pltpu.make_async_copy(
            resid, resid_out.at[pl.ds(core * kept, kept)], local.at[count]
        )
        here.start()
        others = [away, here]
    sums[0] = resid_sq[...]
    sums[1] = jnp.zeros_like(resid_sq)
    tile = min(rows, 128)
    for offset in order:
        fetch(offset).wait()
        for hop in range(1, groups):
            across(offset, hop).wait_recv()

        @pl.loop(0, rows // tile)
        def add(step):
            here = pl.ds(pl.multiple_of(step * tile, tile), tile)
            value = mine[offset, here, :].astype(jnp.float32)
            for hop in range(1, groups):
                value += landed[(hop - 1) * count + offset, here, :].astype(jnp.float32)
            ready[offset, here, :] = value.astype(jnp.bfloat16)
            sums[1] += jnp.sum((value * value).reshape(tile // 8, 8, -1), axis=0)

        if offset:
            direct(offset).start()
    def norm_across(hop):
        there = lax.rem(group + hop, groups)
        return pltpu.make_async_remote_copy(
            src_ref=small,
            dst_ref=sums_y.at[hop - 1],
            send_sem=norm_send.at[count + hop - 1],
            recv_sem=norm_recv.at[count + hop - 1],
            device_id=(freq, there * CORES + core),
            device_id_type=MESH,
        )

    def norm_direct(offset):
        to_freq, _, other = peers_of(freqs, offset, freq, core)
        return pltpu.make_async_remote_copy(
            src_ref=sums_all.at[0],
            dst_ref=sums_all.at[offset],
            send_sem=norm_send.at[offset],
            recv_sem=norm_recv.at[offset],
            device_id=(to_freq, group * CORES + other),
            device_id_type=MESH,
        )

    def folded(value):
        half = value.shape[1] // 2
        value = value[:, :half] + value[:, half:]
        return value[:4] + value[4:]

    small[...] = jnp.concatenate([folded(sums[0]), folded(sums[1])], axis=0)
    for hop in range(1, groups):
        norm_across(hop).start()
    last = pltpu.make_async_copy(ready.at[0], total.at[freq * CORES + core], local.at[count + 1])
    last.start()
    value = small[...]
    for hop in range(1, groups):
        norm_across(hop).wait()
        value = value + sums_y[hop - 1]
    sums_all[0] = value
    for offset in range(1, count):
        norm_direct(offset).start()
    for offset in range(1, count):
        norm_direct(offset).wait()
        value = value + sums_all[offset]
    norms[...] = value
    last.wait()
    for offset in range(1, count):
        direct(offset).wait()
    for hop in range(1, groups):
        for offset in range(count):
            across(offset, hop).wait_send()
    for copy in others:
        copy.wait()


def spread(freqs, groups, ident, spectra, operator=None, data=None):
    count = freqs * CORES
    _, rows, width = spectra.shape
    shapes = [jax.ShapeDtypeStruct((groups * count, rows, width), jnp.bfloat16)]
    dma = pltpu.SemaphoreType.DMA
    sems = [dma((count,)), dma((count,)), dma(((groups - 1) * count,)), dma(((groups - 1) * count,)), dma((3,))]
    args = [spectra]
    if operator is not None:
        kb, two, held, points = operator.shape
        _, kept, _, width = data.shape
        shapes += [
            jax.ShapeDtypeStruct((kb // CORES, two, held, points), jnp.bfloat16),
            jax.ShapeDtypeStruct((kept, held, width), jnp.bfloat16),
        ]
        sems += [dma((SWAPS + 1,)), dma((SWAPS + 1,))]
        args += [operator, data]
    anywhere = pl.BlockSpec(memory_space=pl.ANY)
    return pl.pallas_call(
        functools.partial(spread_kernel, freqs, groups, operator is not None),
        out_shape=shapes,
        in_specs=[anywhere] * len(args),
        out_specs=[anywhere] * len(shapes),
        scratch_shapes=sems,
        compiler_params=pltpu.CompilerParams(
            collective_id=ident, has_side_effects=True, vmem_limit_bytes=VMEM_LIMIT
        ),
    )(*args)


def collect(freqs, groups, ident, part, resid_sq, resid=None, resid_away=None):
    count = freqs * CORES
    _, rows, width = part.shape
    dma = pltpu.SemaphoreType.DMA
    pair = (2,) + resid_sq.shape
    packed = (8, width // 2)
    shapes = [
        jax.ShapeDtypeStruct((count, rows, width), jnp.bfloat16),
        jax.ShapeDtypeStruct(packed, jnp.float32),
    ]
    scratch = [
        pltpu.VMEM(((groups - 1) * count, rows, width), jnp.bfloat16),
        pltpu.VMEM((count, rows, width), jnp.bfloat16),
        pltpu.VMEM((count, rows, width), jnp.bfloat16),
        pltpu.VMEM(pair, jnp.float32),
        pltpu.VMEM(packed, jnp.float32),
        pltpu.VMEM((groups - 1,) + packed, jnp.float32),
        pltpu.VMEM((count,) + packed, jnp.float32),
        dma((count,)), dma((count,)), dma(((groups - 1) * count,)), dma(((groups - 1) * count,)), dma((count + 2,)),
        dma((count + groups - 1,)), dma((count + groups - 1,)),
    ]
    anywhere = pl.BlockSpec(memory_space=pl.ANY)
    outs = [pl.BlockSpec(memory_space=pltpu.VMEM)] * 2
    args = [part, resid_sq]
    if resid is not None:
        kept, held, _ = resid.shape
        shapes.append(jax.ShapeDtypeStruct((kept * CORES, held, width), jnp.bfloat16))
        outs.append(anywhere)
        scratch += [dma((1,)), dma((1,))]
        args += [resid, resid_away]
    return pl.pallas_call(
        functools.partial(collect_kernel, freqs, groups, resid is not None),
        out_shape=shapes,
        in_specs=[anywhere, pl.BlockSpec(memory_space=pltpu.VMEM)] + [anywhere] * (len(args) - 2),
        out_specs=outs,
        scratch_shapes=scratch,
        compiler_params=pltpu.CompilerParams(
            collective_id=ident, has_side_effects=True, vmem_limit_bytes=VMEM_LIMIT
        ),
    )(*args)


def interleave(value, scratch, point, sources, frequencies):
    stride = scratch[0].shape[0] // frequencies
    for which in range(2):
        for part in range(2):
            scratch[part][pl.ds(point + which, frequencies, stride=stride), :] = value[
                part * frequencies : (part + 1) * frequencies,
                which * sources : (which + 1) * sources,
            ]


def write_out(out, scratch, sources):
    tile = 1024

    @pl.loop(0, out.shape[0] // tile)
    def write(step):
        rows = pl.ds(pl.multiple_of(step * tile, tile), tile)
        for part in range(2):
            out[rows, part * sources : (part + 1) * sources] = scratch[part][rows, :].astype(
                jnp.bfloat16
            )


def pair_of(prim):
    return jnp.concatenate([prim[0], prim[1]], axis=1)


def forward_kernel(prim, table, out, *scratch):
    sources = prim.shape[2]
    frequencies = table.shape[0] // 2
    step = pl.program_id(0)
    value = jnp.dot(
        table[...], pair_of(prim).astype(jnp.bfloat16), preferred_element_type=jnp.float32
    )
    interleave(value, scratch, 2 * step, sources, frequencies)

    @pl.when(step == pl.num_programs(0) - 1)
    def finish():
        write_out(out, scratch, sources)


def update_kernel(count_total, last, *refs):
    if last:
        norms, shrink, total, prim, turned_table, prim_out, real, imag = refs
    else:
        norms, shrink, total, prim, turned_table, table, prim_out, out, real, imag, *scratch = refs
    sources = prim.shape[2]
    frequencies = turned_table.shape[1] // 2
    stride = total.shape[0] // frequencies
    step = pl.program_id(0)
    tile = 1024

    @pl.when(step == 0)
    def widen():
        @pl.loop(0, total.shape[0] // tile)
        def copy(step):
            rows = pl.ds(pl.multiple_of(step * tile, tile), tile)
            real[rows, :] = total[rows, :sources].astype(jnp.float32)
            imag[rows, :] = total[rows, sources:].astype(jnp.float32)

    residual_norm = jnp.sum(norms[:4], axis=(0, 1), keepdims=True)
    direction_norm = jnp.sum(norms[4:], axis=(0, 1), keepdims=True)
    step_size = 0.5 * residual_norm / (direction_norm + 1e-06)
    threshold = shrink[...] * (step_size * jnp.sqrt(direction_norm / count_total))
    threshold = jnp.concatenate([threshold, threshold], axis=1)

    def column(point):
        rows = pl.ds(point, frequencies, stride=stride)
        return jnp.concatenate([real[rows, :], imag[rows, :]], axis=0).astype(jnp.bfloat16)

    both = jnp.concatenate([column(2 * step), column(2 * step + 1)], axis=1)
    update = jnp.dot(turned_table[...], both, preferred_element_type=jnp.float32)
    moved = pair_of(prim) + step_size * update
    fresh = moved - jnp.clip(moved, -threshold, threshold)
    prim_out[0] = fresh[:, :sources]
    prim_out[1] = fresh[:, sources:]
    if last:
        return
    value = jnp.dot(table[...], fresh.astype(jnp.bfloat16), preferred_element_type=jnp.float32)
    interleave(value, scratch, 2 * step, sources, frequencies)

    @pl.when(step == pl.num_programs(0) - 1)
    def finish():
        write_out(out, scratch, sources)


def products_kernel(core_ref, near, far, spectra, near_data, far_data, near_res, far_res, part, square):
    batch, _, held, _ = near.shape
    everywhere, _, each, width = spectra.shape
    sources = width // 2

    def product(left, right, side):
        return lax.dot_general(
            left, right, (((side,), (0,)), ((), ())), preferred_element_type=jnp.float32
        )

    def turned(values):
        return jnp.concatenate([-values[:, sources:], values[:, :sources]], axis=1)

    @pl.when(pl.program_id(0) == 0)
    def clear():
        square[...] = jnp.zeros_like(square)

    added = jnp.zeros(square.shape, jnp.float32)
    for k in range(batch):
        values = spectra[:, k].reshape(everywhere * each, width)
        real_op = jnp.concatenate([near[k, 0], far[k, 0]], axis=0)
        imag_op = jnp.concatenate([near[k, 1], far[k, 1]], axis=0)
        predicted = product(real_op, values, 1) + product(imag_op, turned(values), 1)
        recorded = jnp.concatenate([near_data[0, k], far_data[k]], axis=0).astype(jnp.float32)
        resid = (recorded - predicted).astype(jnp.bfloat16)
        near_res[k] = resid[:held]
        far_res[k] = resid[held:]
        wide = resid.astype(jnp.float32)
        added += jnp.sum((wide * wide).reshape(-1, 8, width), axis=0)
        direction = product(real_op, resid, 0) - product(imag_op, turned(resid), 0)
        part[:, k] = direction.astype(jnp.bfloat16).reshape(everywhere, each, width)
    square[...] += added


def params():
    return pltpu.CompilerParams(vmem_limit_bytes=VMEM_LIMIT)


def once(shape):
    return pl.BlockSpec(shape, lambda *_: (0,) * len(shape), pipeline_mode=pl.Buffered(1))


def forward(prim, table):
    points, samples, sources = prim.shape
    rows = table.shape[0] // 2 * points
    return pl.pallas_call(
        forward_kernel,
        grid=(points // 2,),
        out_shape=jax.ShapeDtypeStruct((rows, 2 * sources), jnp.bfloat16),
        in_specs=[pl.BlockSpec((2, samples, sources), lambda i: (i, 0, 0)), once(table.shape)],
        out_specs=once((rows, 2 * sources)),
        scratch_shapes=[pltpu.VMEM((rows, sources), jnp.float32)] * 2,
        compiler_params=params(),
    )(prim, table)


def advance(norms, shrink, total, prim, turned_table, table, count_total, last):
    points, samples, sources = prim.shape
    rows = total.shape[0]
    block = pl.BlockSpec((2, samples, sources), lambda i: (i, 0, 0))
    args = [norms, shrink, total, prim, turned_table]
    specs = [once(norms.shape), once(shrink.shape), once(total.shape), block, once(turned_table.shape)]
    shapes, outs = [jax.ShapeDtypeStruct(prim.shape, jnp.float32)], [block]
    scratch = [pltpu.VMEM((rows, sources), jnp.float32)] * (2 if last else 4)
    if not last:
        args.append(table)
        specs.append(once(table.shape))
        shapes.append(jax.ShapeDtypeStruct(total.shape, jnp.bfloat16))
        outs.append(once(total.shape))
    return pl.pallas_call(
        functools.partial(update_kernel, count_total, last),
        grid=(points // 2,),
        out_shape=shapes,
        in_specs=specs,
        out_specs=outs,
        scratch_shapes=scratch,
        compiler_params=params(),
    )(*args)


def products(core, near, far, spectra, near_data, far_data):
    kept, _, held, _ = far.shape
    everywhere, _, points, width = spectra.shape
    batch = math.gcd(kept, 4)
    rows = pl.BlockSpec((batch, held, width), lambda k, c: (k, 0, 0))
    spread_block = pl.BlockSpec((everywhere, batch, points, width), lambda k, c: (0, k, 0, 0))
    resid_shape = jax.ShapeDtypeStruct((kept, held, width), jnp.bfloat16)
    return pl.pallas_call(
        products_kernel,
        grid_spec=pltpu.PrefetchScalarGridSpec(
            num_scalar_prefetch=1,
            grid=(kept // batch,),
            in_specs=[
                pl.BlockSpec((batch,) + far.shape[1:], lambda k, c: (c[0] * (kept // batch) + k, 0, 0, 0)),
                pl.BlockSpec((batch,) + far.shape[1:], lambda k, c: (k, 0, 0, 0)),
                spread_block,
                pl.BlockSpec((1, batch, held, width), lambda k, c: (c[0], k, 0, 0)),
                rows,
            ],
            out_specs=[rows, rows, spread_block, pl.BlockSpec((8, width), lambda k, c: (0, 0))],
        ),
        out_shape=[
            resid_shape,
            resid_shape,
            jax.ShapeDtypeStruct(spectra.shape, jnp.bfloat16),
            jax.ShapeDtypeStruct((8, width), jnp.float32),
        ],
        compiler_params=params(),
    )(core, near, far, spectra, near_data, far_data)


def plain_forward(prim, table):
    points, samples, sources = prim.shape
    spectra = jnp.einsum(
        "ckt,nts->kncs",
        table.reshape(2, -1, samples),
        prim.astype(jnp.bfloat16),
        preferred_element_type=jnp.float32,
    ).astype(jnp.bfloat16)
    return spectra.reshape(-1, 2 * sources)


def plain_advance(norms, shrink, total, prim, turned_table, table, count_total, last):
    points, samples, sources = prim.shape
    residual_norm, direction_norm = jnp.sum(norms[:4]), jnp.sum(norms[4:])
    step_size = 0.5 * residual_norm / (direction_norm + 1e-06)
    threshold = shrink[:, None, :] * (step_size * jnp.sqrt(direction_norm / count_total))
    update = jnp.einsum(
        "ckt,kncs->nts",
        table.reshape(2, -1, samples),
        total.reshape(-1, points, 2, sources),
        preferred_element_type=jnp.float32,
    )
    moved = prim + step_size * update
    fresh = moved - jnp.clip(moved, -threshold, threshold)
    return (fresh,) if last else (fresh, plain_forward(fresh, table))


def plain_products(core, near, far, spectra, near_data, far_data):
    kept, _, held, _ = far.shape
    everywhere, _, points, width = spectra.shape
    sources = width // 2
    near = lax.dynamic_slice_in_dim(near, core[0] * kept, kept, 0)
    operator = jnp.concatenate([near, far], axis=2)
    near_data = lax.dynamic_index_in_dim(near_data, core[0], 0, keepdims=False)
    recorded = jnp.concatenate([near_data, far_data], axis=1)
    values = spectra.transpose(1, 0, 2, 3).reshape(kept, everywhere * points, width)

    def turned(values):
        return jnp.concatenate([-values[:, :, sources:], values[:, :, :sources]], axis=2)

    def product(order, part, right):
        return jnp.einsum(order, operator[:, part], right, preferred_element_type=jnp.float32)

    ahead, back = "krn,kns->krs", "krn,krs->kns"
    predicted = product(ahead, 0, values) + product(ahead, 1, turned(values))
    resid = (recorded.astype(jnp.float32) - predicted).astype(jnp.bfloat16)
    square = jnp.sum(jnp.square(resid.astype(jnp.float32)).reshape(-1, 8, width), axis=0)
    direction = product(back, 0, resid) - product(back, 1, turned(resid))
    part = direction.astype(jnp.bfloat16).reshape(kept, everywhere, points, width)
    return resid[:, :held], resid[:, held:], part.transpose(1, 0, 2, 3), square


def local(freqs, groups, primaries_start, surface_operator, data_spectra, shrinkage):
    points, samples, sources = primaries_start.shape
    band, _, held, all_points = surface_operator.shape
    kept = band // CORES
    count = freqs * CORES
    everywhere = groups * count
    frequencies = band * freqs
    width = 2 * sources
    rows = transform_table(frequencies, samples)
    table, turned_table = jnp.asarray(rows), jnp.asarray(np.ascontiguousarray(rows.T))
    primaries = primaries_start
    count_total = 2.0 * frequencies * all_points * sources
    whole_tiles = points % 16 == 0
    go_forward, go_advance, multiply = (
        (forward, advance, products)
        if whole_tiles
        else (plain_forward, plain_advance, plain_products)
    )

    core = lax.rem(lax.axis_index("rcv"), CORES).astype(jnp.int32).reshape(1)
    data = data_spectra.reshape(held, CORES, kept, width).transpose(1, 2, 0, 3)
    shrink = shrinkage.reshape(1, sources)
    local_spectra = go_forward(primaries, table)
    for iteration in range(ITERS):
        last = iteration == ITERS - 1
        message = local_spectra.reshape(count, kept * points, width)
        if iteration == 0:
            spectra, far, far_data = spread(freqs, groups, 0, message, surface_operator, data)
        else:
            (spectra,) = spread(freqs, groups, 2, message)
        near_res, far_res, part, square = multiply(
            core,
            surface_operator,
            far,
            spectra.reshape(everywhere, kept, points, width),
            data,
            far_data,
        )
        part = part.reshape(everywhere, kept * points, width)
        if not last:
            total, norms = collect(freqs, groups, 1, part, square)
        else:
            total, norms, residual = collect(freqs, groups, 3, part, square, near_res, far_res)
        total = total.reshape(frequencies * points, width)
        primaries, *more = go_advance(
            norms, shrink, total, primaries, turned_table, table, count_total, last
        )
        if more:
            (local_spectra,) = more
    residual = residual.transpose(1, 0, 2).reshape(held, band, 2, sources)
    return (primaries, residual)


def solution(mesh):
    freqs = mesh.shape["freq"]
    groups = mesh.shape["rcv"] // CORES
    return jax.shard_map(
        functools.partial(local, freqs, groups),
        mesh=mesh,
        in_specs=(
            P(("rcv", "freq"), None, None),
            P("freq", None, "rcv", None),
            P("rcv", "freq", None, None),
            P(),
        ),
        out_specs=(P(("rcv", "freq"), None, None), P("rcv", "freq", None, None)),
        check_vma=False,
    )
```

```python
import functools
import math

import jax
import jax.numpy as jnp
import numpy as np
from jax import lax
from jax.experimental import pallas as pl
from jax.experimental.pallas import tpu as pltpu
from jax.sharding import PartitionSpec as P

ITERS = 2
CORES = 2
SWAPS = 8
BATCH = 4
MESH = pl.DeviceIdType.MESH
VMEM_LIMIT = 56 * 1024 * 1024


def transform_table(frequencies, samples):
    phase = np.arange(frequencies)[:, None] * np.arange(samples)[None, :] % samples
    angle = phase * (2.0 * math.pi / samples)
    factor = math.sqrt(2.0 / samples)
    rows = np.concatenate([factor * np.cos(angle), -factor * np.sin(angle)], axis=0)
    return rows.astype(np.float32).astype(jnp.bfloat16)


def place(groups):
    freq = lax.axis_index("freq")
    rcv = lax.axis_index("rcv")
    return freq, rcv // CORES, lax.rem(rcv, CORES)


def peers_of(freqs, offset, freq, core):
    step, flip = offset // CORES, offset % CORES
    to_freq = lax.rem(freq + step, freqs)
    from_freq = lax.rem(freq + freqs - step, freqs)
    other = lax.rem(core + flip, CORES)
    return to_freq, from_freq, other


def far_first(freqs):
    steps = sorted(range(freqs), key=lambda step: (abs(step - freqs // 2), step))
    return [step * CORES + flip for step in steps for flip in range(CORES - 1, -1, -1)]


def mixed(freqs):
    steps = sorted(range(1, freqs), key=lambda step: (abs(step - freqs // 2), step))
    turn = []
    while steps:
        turn.append(steps.pop(0))
        if steps:
            turn.append(steps.pop(-1))
    return [1] + [step * CORES + flip for step in turn for flip in range(CORES)]


def enter(freqs, groups, freq, group, core):
    barrier = pltpu.get_barrier_semaphore()
    for offset in range(1, freqs * CORES):
        to_freq, _, other = peers_of(freqs, offset, freq, core)
        pl.semaphore_signal(
            barrier, inc=1, device_id=(to_freq, group * CORES + other), device_id_type=MESH
        )
    for hop in range(1, groups):
        there = lax.rem(group + hop, groups)
        pl.semaphore_signal(
            barrier, inc=1, device_id=(freq, there * CORES + core), device_id_type=MESH
        )
    pl.semaphore_wait(barrier, freqs * CORES - 1 + groups - 1)


def spread_kernel(freqs, groups, with_operator, *refs):
    if with_operator:
        spec, oper, data, gathered, oper_out, data_out, *sems = refs
        send, recv, send_y, recv_y, local, swap_send, swap_recv = sems
    else:
        spec, gathered, send, recv, send_y, recv_y, local = refs
    freq, group, core = place(groups)
    count = freqs * CORES
    enter(freqs, groups, freq, group, core)

    def slot(source_freq, source_core, source_group=group):
        return (source_group * CORES + source_core) * freqs + source_freq

    def direct(offset):
        to_freq, _, other = peers_of(freqs, offset, freq, core)
        return pltpu.make_async_remote_copy(
            src_ref=spec.at[to_freq * CORES + other],
            dst_ref=gathered.at[slot(freq, core)],
            send_sem=send.at[offset],
            recv_sem=recv.at[offset],
            device_id=(to_freq, group * CORES + other),
            device_id_type=MESH,
        )

    def forward(offset, hop):
        _, from_freq, other = peers_of(freqs, offset, freq, core)
        there = lax.rem(group + hop, groups)
        place_of = slot(from_freq, other)
        source = spec.at[freq * CORES + core] if offset == 0 else gathered.at[place_of]
        return pltpu.make_async_remote_copy(
            src_ref=source,
            dst_ref=gathered.at[place_of],
            send_sem=send_y.at[(hop - 1) * count + offset],
            recv_sem=recv_y.at[(hop - 1) * count + offset],
            device_id=(freq, there * CORES + core),
            device_id_type=MESH,
        )

    order = mixed(freqs)
    for offset in order:
        direct(offset).start()
    own = pltpu.make_async_copy(
        spec.at[freq * CORES + core], gathered.at[slot(freq, core)], local.at[0]
    )
    own.start()
    for hop in range(1, groups):
        forward(0, hop).start()
    others = []
    if with_operator:
        sibling = 1 - core
        kept = oper_out.shape[0]
        size = kept // SWAPS
        pieces = [(data.at[sibling], data_out)]
        for piece in range(SWAPS):
            pieces.append(
                (
                    oper.at[pl.ds(sibling * kept + piece * size, size)],
                    oper_out.at[pl.ds(piece * size, size)],
                )
            )
        for number, (source, target) in enumerate(pieces):
            away = pltpu.make_async_remote_copy(
                src_ref=source,
                dst_ref=target,
                send_sem=swap_send.at[number],
                recv_sem=swap_recv.at[number],
                device_id=(freq, group * CORES + sibling),
                device_id_type=MESH,
            )
            away.start()
            others.append(away)
    for offset in order:
        direct(offset).wait_recv()
        for hop in range(1, groups):
            forward(offset, hop).start()
    own.wait()
    for offset in order:
        direct(offset).wait_send()
    for hop in range(1, groups):
        for offset in range(count):
            forward(offset, hop).wait()
    for copy in others:
        copy.wait()


def collect_kernel(freqs, groups, with_residual, *refs):
    if with_residual:
        part, resid_sq, resid, resid_away, total, norms, resid_out, *rest = refs
        *rest, swap_send, swap_recv = rest
    else:
        part, resid_sq, total, norms, *rest = refs
    landed, ready, mine, sums, small, sums_y, sums_all, *rest = rest
    send, recv, send_y, recv_y, local, norm_send, norm_recv = rest
    freq, group, core = place(groups)
    count = freqs * CORES
    rows = part.shape[1]
    enter(freqs, groups, freq, group, core)

    def slot(freq_of, core_of, group_of):
        return (group_of * CORES + core_of) * freqs + freq_of

    def across(offset, hop):
        to_freq, _, other = peers_of(freqs, offset, freq, core)
        there = lax.rem(group + hop, groups)
        number = (hop - 1) * count + offset
        return pltpu.make_async_remote_copy(
            src_ref=part.at[slot(to_freq, other, there)],
            dst_ref=landed.at[number],
            send_sem=send_y.at[number],
            recv_sem=recv_y.at[number],
            device_id=(freq, there * CORES + core),
            device_id_type=MESH,
        )

    def fetch(offset):
        to_freq, _, other = peers_of(freqs, offset, freq, core)
        return pltpu.make_async_copy(
            part.at[slot(to_freq, other, group)], mine.at[offset], local.at[offset]
        )

    def direct(offset):
        to_freq, _, other = peers_of(freqs, offset, freq, core)
        return pltpu.make_async_remote_copy(
            src_ref=ready.at[offset],
            dst_ref=total.at[freq * CORES + core],
            send_sem=send.at[offset],
            recv_sem=recv.at[offset],
            device_id=(to_freq, group * CORES + other),
            device_id_type=MESH,
        )

    order = far_first(freqs)
    others = []
    for offset in order:
        for hop in range(1, groups):
            across(offset, hop).start()
        fetch(offset).start()
    if with_residual:
        sibling = 1 - core
        kept = resid.shape[0]
        away = pltpu.make_async_remote_copy(
            src_ref=resid_away,
            dst_ref=resid_out.at[pl.ds(core * kept, kept)],
            send_sem=swap_send.at[0],
            recv_sem=swap_recv.at[0],
            device_id=(freq, group * CORES + sibling),
            device_id_type=MESH,
        )
        away.start()
        here = pltpu.make_async_copy(
            resid, resid_out.at[pl.ds(core * kept, kept)], local.at[count]
        )
        here.start()
        others = [away, here]
    sums[0] = resid_sq[...]
    sums[1] = jnp.zeros_like(resid_sq)
    tile = min(rows, 128)
    for offset in order:
        fetch(offset).wait()
        for hop in range(1, groups):
            across(offset, hop).wait_recv()

        @pl.loop(0, rows // tile)
        def add(step):
            here = pl.ds(pl.multiple_of(step * tile, tile), tile)
            value = mine[offset, here, :].astype(jnp.float32)
            for hop in range(1, groups):
                value += landed[(hop - 1) * count + offset, here, :].astype(jnp.float32)
            ready[offset, here, :] = value.astype(jnp.bfloat16)
            sums[1] += jnp.sum((value * value).reshape(tile // 8, 8, -1), axis=0)

        if offset:
            direct(offset).start()
    def norm_across(hop):
        there = lax.rem(group + hop, groups)
        return pltpu.make_async_remote_copy(
            src_ref=small,
            dst_ref=sums_y.at[hop - 1],
            send_sem=norm_send.at[count + hop - 1],
            recv_sem=norm_recv.at[count + hop - 1],
            device_id=(freq, there * CORES + core),
            device_id_type=MESH,
        )

    def norm_direct(offset):
        to_freq, _, other = peers_of(freqs, offset, freq, core)
        return pltpu.make_async_remote_copy(
            src_ref=sums_all.at[0],
            dst_ref=sums_all.at[offset],
            send_sem=norm_send.at[offset],
            recv_sem=norm_recv.at[offset],
            device_id=(to_freq, group * CORES + other),
            device_id_type=MESH,
        )

    def folded(value):
        half = value.shape[1] // 2
        value = value[:, :half] + value[:, half:]
        return value[:4] + value[4:]

    small[...] = jnp.concatenate([folded(sums[0]), folded(sums[1])], axis=0)
    for hop in range(1, groups):
        norm_across(hop).start()
    last = pltpu.make_async_copy(ready.at[0], total.at[freq * CORES + core], local.at[count + 1])
    last.start()
    value = small[...]
    for hop in range(1, groups):
        norm_across(hop).wait()
        value = value + sums_y[hop - 1]
    sums_all[0] = value
    for offset in range(1, count):
        norm_direct(offset).start()
    for offset in range(1, count):
        norm_direct(offset).wait()
        value = value + sums_all[offset]
    norms[...] = value
    last.wait()
    for offset in range(1, count):
        direct(offset).wait()
    for hop in range(1, groups):
        for offset in range(count):
            across(offset, hop).wait_send()
    for copy in others:
        copy.wait()


def spread(freqs, groups, ident, spectra, operator=None, data=None):
    count = freqs * CORES
    _, rows, width = spectra.shape
    shapes = [jax.ShapeDtypeStruct((groups * count, rows, width), jnp.bfloat16)]
    dma = pltpu.SemaphoreType.DMA
    sems = [dma((count,)), dma((count,)), dma(((groups - 1) * count,)), dma(((groups - 1) * count,)), dma((3,))]
    args = [spectra]
    if operator is not None:
        kb, two, held, points = operator.shape
        _, kept, _, width = data.shape
        shapes += [
            jax.ShapeDtypeStruct((kb // CORES, two, held, points), jnp.bfloat16),
            jax.ShapeDtypeStruct((kept, held, width), jnp.bfloat16),
        ]
        sems += [dma((SWAPS + 1,)), dma((SWAPS + 1,))]
        args += [operator, data]
    anywhere = pl.BlockSpec(memory_space=pl.ANY)
    held_in = pl.BlockSpec(memory_space=pltpu.VMEM)
    return pl.pallas_call(
        functools.partial(spread_kernel, freqs, groups, operator is not None),
        out_shape=shapes,
        in_specs=[held_in] + [anywhere] * (len(args) - 1),
        out_specs=[held_in] + [anywhere] * (len(shapes) - 1),
        scratch_shapes=sems,
        compiler_params=pltpu.CompilerParams(
            collective_id=ident, has_side_effects=True, vmem_limit_bytes=VMEM_LIMIT
        ),
    )(*args)


def collect(freqs, groups, ident, part, resid_sq, resid=None, resid_away=None):
    count = freqs * CORES
    _, rows, width = part.shape
    dma = pltpu.SemaphoreType.DMA
    pair = (2,) + resid_sq.shape
    packed = (8, width // 2)
    shapes = [
        jax.ShapeDtypeStruct((count, rows, width), jnp.bfloat16),
        jax.ShapeDtypeStruct(packed, jnp.float32),
    ]
    scratch = [
        pltpu.VMEM(((groups - 1) * count, rows, width), jnp.bfloat16),
        pltpu.VMEM((count, rows, width), jnp.bfloat16),
        pltpu.VMEM((count, rows, width), jnp.bfloat16),
        pltpu.VMEM(pair, jnp.float32),
        pltpu.VMEM(packed, jnp.float32),
        pltpu.VMEM((groups - 1,) + packed, jnp.float32),
        pltpu.VMEM((count,) + packed, jnp.float32),
        dma((count,)), dma((count,)), dma(((groups - 1) * count,)), dma(((groups - 1) * count,)), dma((count + 2,)),
        dma((count + groups - 1,)), dma((count + groups - 1,)),
    ]
    anywhere = pl.BlockSpec(memory_space=pl.ANY)
    outs = [pl.BlockSpec(memory_space=pltpu.VMEM)] * 2
    args = [part, resid_sq]
    if resid is not None:
        kept, held, _ = resid.shape
        shapes.append(jax.ShapeDtypeStruct((kept * CORES, held, width), jnp.bfloat16))
        outs.append(anywhere)
        scratch += [dma((1,)), dma((1,))]
        args += [resid, resid_away]
    return pl.pallas_call(
        functools.partial(collect_kernel, freqs, groups, resid is not None),
        out_shape=shapes,
        in_specs=[anywhere, pl.BlockSpec(memory_space=pltpu.VMEM)] + [anywhere] * (len(args) - 2),
        out_specs=outs,
        scratch_shapes=scratch,
        compiler_params=pltpu.CompilerParams(
            collective_id=ident, has_side_effects=True, vmem_limit_bytes=VMEM_LIMIT
        ),
    )(*args)


def interleave(value, scratch, point, sources, frequencies):
    stride = scratch[0].shape[0] // frequencies
    for which in range(2):
        for part in range(2):
            scratch[part][pl.ds(point + which, frequencies, stride=stride), :] = value[
                part * frequencies : (part + 1) * frequencies,
                which * sources : (which + 1) * sources,
            ]


def write_out(out, scratch, sources):
    tile = 1024

    @pl.loop(0, out.shape[0] // tile)
    def write(step):
        rows = pl.ds(pl.multiple_of(step * tile, tile), tile)
        for part in range(2):
            out[rows, part * sources : (part + 1) * sources] = scratch[part][rows, :].astype(
                jnp.bfloat16
            )


def pair_of(prim, first):
    return jnp.concatenate([prim[first], prim[first + 1]], axis=1)


def forward_kernel(prim, table, out, *scratch):
    sources = prim.shape[2]
    frequencies = table.shape[0] // 2
    step = pl.program_id(0)
    batch = prim.shape[0]
    for first in range(0, batch, 2):
        value = jnp.dot(
            table[...],
            pair_of(prim, first).astype(jnp.bfloat16),
            preferred_element_type=jnp.float32,
        )
        interleave(value, scratch, batch * step + first, sources, frequencies)

    @pl.when(step == pl.num_programs(0) - 1)
    def finish():
        write_out(out, scratch, sources)


def update_kernel(count_total, last, *refs):
    if last:
        norms, shrink, total, prim, turned_table, prim_out, real, imag = refs
    else:
        norms, shrink, total, prim, turned_table, table, prim_out, out, real, imag, *scratch = refs
    sources = prim.shape[2]
    frequencies = turned_table.shape[1] // 2
    stride = total.shape[0] // frequencies
    step = pl.program_id(0)
    tile = 1024

    @pl.when(step == 0)
    def widen():
        @pl.loop(0, total.shape[0] // tile)
        def copy(step):
            rows = pl.ds(pl.multiple_of(step * tile, tile), tile)
            real[rows, :] = total[rows, :sources].astype(jnp.float32)
            imag[rows, :] = total[rows, sources:].astype(jnp.float32)

    residual_norm = jnp.sum(norms[:4], axis=(0, 1), keepdims=True)
    direction_norm = jnp.sum(norms[4:], axis=(0, 1), keepdims=True)
    step_size = 0.5 * residual_norm / (direction_norm + 1e-06)
    threshold = shrink[...] * (step_size * jnp.sqrt(direction_norm / count_total))
    threshold = jnp.concatenate([threshold, threshold], axis=1)

    def column(point):
        rows = pl.ds(point, frequencies, stride=stride)
        return jnp.concatenate([real[rows, :], imag[rows, :]], axis=0).astype(jnp.bfloat16)

    batch = prim.shape[0]
    for first in range(0, batch, 2):
        point = batch * step + first
        both = jnp.concatenate([column(point), column(point + 1)], axis=1)
        update = jnp.dot(turned_table[...], both, preferred_element_type=jnp.float32)
        moved = pair_of(prim, first) + step_size * update
        fresh = moved - jnp.clip(moved, -threshold, threshold)
        prim_out[first] = fresh[:, :sources]
        prim_out[first + 1] = fresh[:, sources:]
        if not last:
            value = jnp.dot(
                table[...], fresh.astype(jnp.bfloat16), preferred_element_type=jnp.float32
            )
            interleave(value, scratch, point, sources, frequencies)
    if last:
        return

    @pl.when(step == pl.num_programs(0) - 1)
    def finish():
        write_out(out, scratch, sources)


def products_kernel(core_ref, near, far, spectra, near_data, far_data, near_res, far_res, part, square):
    batch, _, held, _ = near.shape
    everywhere, _, each, width = spectra.shape
    sources = width // 2

    def product(left, right, side):
        return lax.dot_general(
            left, right, (((side,), (0,)), ((), ())), preferred_element_type=jnp.float32
        )

    def turned(values):
        return jnp.concatenate([-values[:, sources:], values[:, :sources]], axis=1)

    @pl.when(pl.program_id(0) == 0)
    def clear():
        square[...] = jnp.zeros_like(square)

    added = jnp.zeros(square.shape, jnp.float32)
    for k in range(batch):
        values = spectra[:, k].reshape(everywhere * each, width)
        real_op = jnp.concatenate([near[k, 0], far[k, 0]], axis=0)
        imag_op = jnp.concatenate([near[k, 1], far[k, 1]], axis=0)
        predicted = product(real_op, values, 1) + product(imag_op, turned(values), 1)
        recorded = jnp.concatenate([near_data[0, k], far_data[k]], axis=0).astype(jnp.float32)
        resid = (recorded - predicted).astype(jnp.bfloat16)
        near_res[k] = resid[:held]
        far_res[k] = resid[held:]
        wide = resid.astype(jnp.float32)
        added += jnp.sum((wide * wide).reshape(-1, 8, width), axis=0)
        direction = product(real_op, resid, 0) - product(imag_op, turned(resid), 0)
        part[:, k] = direction.astype(jnp.bfloat16).reshape(everywhere, each, width)
    square[...] += added


def params():
    return pltpu.CompilerParams(vmem_limit_bytes=VMEM_LIMIT)


def once(shape):
    return pl.BlockSpec(shape, lambda *_: (0,) * len(shape), pipeline_mode=pl.Buffered(1))


def forward(prim, table):
    points, samples, sources = prim.shape
    rows = table.shape[0] // 2 * points
    return pl.pallas_call(
        forward_kernel,
        grid=(points // BATCH,),
        out_shape=jax.ShapeDtypeStruct((rows, 2 * sources), jnp.bfloat16),
        in_specs=[pl.BlockSpec((BATCH, samples, sources), lambda i: (i, 0, 0)), once(table.shape)],
        out_specs=once((rows, 2 * sources)),
        scratch_shapes=[pltpu.VMEM((rows, sources), jnp.float32)] * 2,
        compiler_params=params(),
    )(prim, table)


def advance(norms, shrink, total, prim, turned_table, table, count_total, last):
    points, samples, sources = prim.shape
    rows = total.shape[0]
    block = pl.BlockSpec((BATCH, samples, sources), lambda i: (i, 0, 0))
    args = [norms, shrink, total, prim, turned_table]
    specs = [once(norms.shape), once(shrink.shape), once(total.shape), block, once(turned_table.shape)]
    shapes, outs = [jax.ShapeDtypeStruct(prim.shape, jnp.float32)], [block]
    scratch = [pltpu.VMEM((rows, sources), jnp.float32)] * (2 if last else 4)
    if not last:
        args.append(table)
        specs.append(once(table.shape))
        shapes.append(jax.ShapeDtypeStruct(total.shape, jnp.bfloat16))
        outs.append(once(total.shape))
    return pl.pallas_call(
        functools.partial(update_kernel, count_total, last),
        grid=(points // BATCH,),
        out_shape=shapes,
        in_specs=specs,
        out_specs=outs,
        scratch_shapes=scratch,
        compiler_params=params(),
    )(*args)


def products(core, near, far, spectra, near_data, far_data):
    kept, _, held, _ = far.shape
    everywhere, _, points, width = spectra.shape
    batch = math.gcd(kept, 4)
    rows = pl.BlockSpec((batch, held, width), lambda k, c: (k, 0, 0))
    spread_block = pl.BlockSpec((everywhere, batch, points, width), lambda k, c: (0, k, 0, 0))
    resid_shape = jax.ShapeDtypeStruct((kept, held, width), jnp.bfloat16)
    return pl.pallas_call(
        products_kernel,
        grid_spec=pltpu.PrefetchScalarGridSpec(
            num_scalar_prefetch=1,
            grid=(kept // batch,),
            in_specs=[
                pl.BlockSpec((batch,) + far.shape[1:], lambda k, c: (c[0] * (kept // batch) + k, 0, 0, 0)),
                pl.BlockSpec((batch,) + far.shape[1:], lambda k, c: (k, 0, 0, 0)),
                spread_block,
                pl.BlockSpec((1, batch, held, width), lambda k, c: (c[0], k, 0, 0)),
                rows,
            ],
            out_specs=[rows, rows, spread_block, pl.BlockSpec((8, width), lambda k, c: (0, 0))],
        ),
        out_shape=[
            resid_shape,
            resid_shape,
            jax.ShapeDtypeStruct(spectra.shape, jnp.bfloat16),
            jax.ShapeDtypeStruct((8, width), jnp.float32),
        ],
        compiler_params=params(),
    )(core, near, far, spectra, near_data, far_data)


def plain_forward(prim, table):
    points, samples, sources = prim.shape
    spectra = jnp.einsum(
        "ckt,nts->kncs",
        table.reshape(2, -1, samples),
        prim.astype(jnp.bfloat16),
        preferred_element_type=jnp.float32,
    ).astype(jnp.bfloat16)
    return spectra.reshape(-1, 2 * sources)


def plain_advance(norms, shrink, total, prim, turned_table, table, count_total, last):
    points, samples, sources = prim.shape
    residual_norm, direction_norm = jnp.sum(norms[:4]), jnp.sum(norms[4:])
    step_size = 0.5 * residual_norm / (direction_norm + 1e-06)
    threshold = shrink[:, None, :] * (step_size * jnp.sqrt(direction_norm / count_total))
    update = jnp.einsum(
        "ckt,kncs->nts",
        table.reshape(2, -1, samples),
        total.reshape(-1, points, 2, sources),
        preferred_element_type=jnp.float32,
    )
    moved = prim + step_size * update
    fresh = moved - jnp.clip(moved, -threshold, threshold)
    return (fresh,) if last else (fresh, plain_forward(fresh, table))


def plain_products(core, near, far, spectra, near_data, far_data):
    kept, _, held, _ = far.shape
    everywhere, _, points, width = spectra.shape
    sources = width // 2
    near = lax.dynamic_slice_in_dim(near, core[0] * kept, kept, 0)
    operator = jnp.concatenate([near, far], axis=2)
    near_data = lax.dynamic_index_in_dim(near_data, core[0], 0, keepdims=False)
    recorded = jnp.concatenate([near_data, far_data], axis=1)
    values = spectra.transpose(1, 0, 2, 3).reshape(kept, everywhere * points, width)

    def turned(values):
        return jnp.concatenate([-values[:, :, sources:], values[:, :, :sources]], axis=2)

    def product(order, part, right):
        return jnp.einsum(order, operator[:, part], right, preferred_element_type=jnp.float32)

    ahead, back = "krn,kns->krs", "krn,krs->kns"
    predicted = product(ahead, 0, values) + product(ahead, 1, turned(values))
    resid = (recorded.astype(jnp.float32) - predicted).astype(jnp.bfloat16)
    square = jnp.sum(jnp.square(resid.astype(jnp.float32)).reshape(-1, 8, width), axis=0)
    direction = product(back, 0, resid) - product(back, 1, turned(resid))
    part = direction.astype(jnp.bfloat16).reshape(kept, everywhere, points, width)
    return resid[:, :held], resid[:, held:], part.transpose(1, 0, 2, 3), square


def local(freqs, groups, primaries_start, surface_operator, data_spectra, shrinkage):
    points, samples, sources = primaries_start.shape
    band, _, held, all_points = surface_operator.shape
    kept = band // CORES
    count = freqs * CORES
    everywhere = groups * count
    frequencies = band * freqs
    width = 2 * sources
    rows = transform_table(frequencies, samples)
    table, turned_table = jnp.asarray(rows), jnp.asarray(np.ascontiguousarray(rows.T))
    primaries = primaries_start
    count_total = 2.0 * frequencies * all_points * sources
    whole_tiles = points % 16 == 0
    go_forward, go_advance, multiply = (
        (forward, advance, products)
        if whole_tiles
        else (plain_forward, plain_advance, plain_products)
    )

    core = lax.rem(lax.axis_index("rcv"), CORES).astype(jnp.int32).reshape(1)
    data = data_spectra.reshape(held, CORES, kept, width).transpose(1, 2, 0, 3)
    shrink = shrinkage.reshape(1, sources)
    local_spectra = go_forward(primaries, table)
    for iteration in range(ITERS):
        last = iteration == ITERS - 1
        message = local_spectra.reshape(count, kept * points, width)
        if iteration == 0:
            spectra, far, far_data = spread(freqs, groups, 0, message, surface_operator, data)
        else:
            (spectra,) = spread(freqs, groups, 2, message)
        near_res, far_res, part, square = multiply(
            core,
            surface_operator,
            far,
            spectra.reshape(everywhere, kept, points, width),
            data,
            far_data,
        )
        part = part.reshape(everywhere, kept * points, width)
        if not last:
            total, norms = collect(freqs, groups, 1, part, square)
        else:
            total, norms, residual = collect(freqs, groups, 3, part, square, near_res, far_res)
        total = total.reshape(frequencies * points, width)
        primaries, *more = go_advance(
            norms, shrink, total, primaries, turned_table, table, count_total, last
        )
        if more:
            (local_spectra,) = more
    residual = residual.transpose(1, 0, 2).reshape(held, band, 2, sources)
    return (primaries, residual)


def solution(mesh):
    freqs = mesh.shape["freq"]
    groups = mesh.shape["rcv"] // CORES
    return jax.shard_map(
        functools.partial(local, freqs, groups),
        mesh=mesh,
        in_specs=(
            P(("rcv", "freq"), None, None),
            P("freq", None, "rcv", None),
            P("rcv", "freq", None, None),
            P(),
        ),
        out_specs=(P(("rcv", "freq"), None, None), P("rcv", "freq", None, None)),
        check_vma=False,
    )
```
